32 devices in a mesh: sys: 2 (over x), slab: 16 (over z, y, core).
Axes of the slice: x: 2, y: 2, z: 4, core: 2. Of those that a mesh axis runs over, the one named last changes fastest.
Arguments:
- correlation: float32 [24, 256, 32, 256], P('sys', 'slab'), parts along dimension 0, may hold values from -6 to 6
- lj_field: float32 [12, 256, 32, 256], P('sys', 'slab'), parts along dimension 0, may hold values from -1 to 3
- potential: float32 [512, 32, 256], P(('sys', 'slab')), parts along dimension 0, may hold values from -8 to 8
- species: int32 [12], replicated, may hold values from 0 to 5
- charges: int32 [12], replicated, may hold values from -2 to 2
- chi_amp: float32 [3, 12, 12], replicated, may hold values from -2.4 to 2.4
- chi_width: float32 [3], replicated, may hold values from 0.05 to 2
Outputs:
- total_corr: float32 [24, 256, 32, 256], P('sys', 'slab'), parts along dimension 0
- next_corr: float32 [24, 256, 32, 256], P('sys', 'slab'), parts along dimension 0
- residual_rms: float32 [2], P('sys'), parts along dimension 0
The draws below stay inside these ranges and needn't reach their ends.
There are 2 independent parts, one for each index of `sys`. The reference program is written for one: setup_inputs(seed, part) draws one part's arguments, and reference() takes and returns one part's arrays. A program takes and returns all parts, laid end to end along the dimension named above; an argument that names none is the same for every part. Nothing has to cross between parts.
All inputs are finite; a program needn't handle non-finite values.
Results may differ from the reference program's by a relative error of at most 0.0003.
Values sent between devices are 32-bit elements; how exact they have to be, the bound alone decides.
A program may use at most 320 MiB of HBM per device.

```python
import math
import jax
import jax.numpy as jnp
from jax import lax

SITES = 12
SPECIES = 6
TERMS = 3
NA = 256
NZ = 32
NB = 256


def draw_potential(key, part):
    key = jax.random.fold_in(key, 7)
    placing = jnp.arange(NA).astype(jnp.float32) / (NA - 1)
    values = jnp.clip(jax.random.normal(key, (NA, NZ, NB), jnp.float32), -5.0, 5.0)
    growth = 1.0 + 2.0 * placing
    return (0.5 * growth[:, None, None] * values).astype(jnp.float32)


def draw_correlation(key, part):
    key = jax.random.fold_in(key, 11)
    noise_key, scale_key, phase_key = jax.random.split(key, 3)
    row_ids = jnp.arange(NA).astype(jnp.int32)
    col_ids = jnp.arange(NB).astype(jnp.int32)
    parity = (1 - 2 * (row_ids % 2)).astype(jnp.float32)
    phases = jax.random.uniform(phase_key, (SITES, 2), jnp.float32, 0.0, 1.0)
    noise_part = 0.6 * jnp.clip(jax.random.normal(noise_key, (SITES, NA, NZ, NB), jnp.float32), -3.0, 3.0)
    site_scale = jax.random.uniform(scale_key, (SITES,), jnp.float32, 0.8, 1.2)
    wave_rows = 1.5 + jnp.cos(2.0 * math.pi * (row_ids.astype(jnp.float32)[None, :] / NA + phases[:, 0:1]))
    wave_cols = 1.0 + 0.3 * jnp.cos(2.0 * math.pi * (col_ids.astype(jnp.float32)[None, :] / NB + phases[:, 1:2]))
    smooth_part = site_scale[:, None, None, None] * (parity[None, :] * wave_rows)[:, :, None, None] * wave_cols[:, None, None, :]
    return (noise_part + smooth_part).astype(jnp.float32)


def draw_chi_width(key, part):
    key = jax.random.fold_in(key, 13)
    pick_key, base_key, near_key = jax.random.split(key, 3)
    picked = jax.random.randint(pick_key, (), 0, TERMS)
    base_widths = jnp.exp(jax.random.uniform(base_key, (TERMS,), jnp.float32, math.log(0.05), math.log(2.0)))
    near_width = jax.random.uniform(near_key, (), jnp.float32, 0.07, 0.15)
    term_ids = jnp.arange(TERMS).astype(jnp.int32)
    return jnp.where(term_ids == picked, near_width, base_widths).astype(jnp.float32)


def plant(entries, own_key, low, largest):
    longest = entries.shape.index(max(entries.shape))
    spots = []
    for shift in (0, 1):
        where = [jax.random.randint(jax.random.fold_in(own_key, axis), (), 0, length) for axis, length in enumerate(entries.shape)]
        where[longest] = (where[longest] + shift) % entries.shape[longest]
        spots.append(tuple(where))
    return entries.at[spots[0]].set(low).at[spots[1]].set(largest)


def steps_of(stream_key, shape, cuts, low, high):
    def one(position, blocks):
        heights = jax.random.uniform(jax.random.fold_in(jax.random.fold_in(stream_key, 6), position), (blocks,), jnp.float32, low / len(cuts), high / len(cuts))
        return jnp.repeat(jnp.exp(heights), shape[position] // blocks).reshape((-1,) + (1,) * (len(shape) - position - 1))

    factor_of = one(*cuts[0])
    for cut in cuts[1:]:
        factor_of = factor_of * one(*cut)
    return factor_of


def scatter_about(rng, dims, spread, bound, kind=jnp.bfloat16):
    array = jax.random.normal(rng, dims, jnp.float32) * spread
    return jnp.minimum(jnp.maximum(array, -bound), bound).astype(kind)


def setup_inputs(seed: int = 0, part: int = 0) -> dict:
    streams_of = jax.random.split(jax.random.key(seed), 8)
    part_splits = jax.random.split(jax.random.fold_in(streams_of[7], part), 8)
    return {
        "correlation": draw_correlation(jax.random.fold_in(jax.random.fold_in(streams_of[7], part), 71), part),
        "lj_field": jnp.clip(-1.0 + 4.0 * jax.random.uniform(part_splits[1], (SPECIES, NA, NZ, NB), jnp.float32) ** steps_of(part_splits[1], (SPECIES, NA, NZ, NB), ((1, 16),), -0.2, 0.2), -1.0, 3.0),
        "potential": draw_potential(jax.random.fold_in(jax.random.fold_in(streams_of[7], part), 71), part),
        "species": plant(jax.random.randint(streams_of[3], (SITES,), 0, SPECIES), jax.random.fold_in(streams_of[3], 1), 0, SPECIES - 1).astype(jnp.int32),
        "charges": plant(jax.random.randint(streams_of[4], (SITES,), -2, 3), jax.random.fold_in(streams_of[4], 1), -2, 2).astype(jnp.int32),
        "chi_amp": scatter_about(streams_of[5], (TERMS, SITES, SITES), 0.4, 2.4, jnp.float32),
        "chi_width": draw_chi_width(jax.random.fold_in(streams_of[7], 71), part),
    }


def signed_freq(count, total):
    index = jnp.arange(count).astype(jnp.int32)
    return ((index + total // 2) % total - total // 2).astype(jnp.float32) / total

def reference(correlation, lj_field, potential, species, charges, chi_amp, chi_width):
    spectrum = jnp.fft.rfftn(correlation, axes=(1, 2, 3))
    spec_real = jnp.real(spectrum)
    spec_imag = jnp.imag(spectrum)
    along_a = signed_freq(NA, NA)[:, None, None]
    along_z = signed_freq(NZ, NZ)[None, :, None]
    along_b = signed_freq(NB // 2 + 1, NB)[None, None, :]
    ksquare = (2.0 * math.pi) ** 2 * (along_a * along_a + along_z * along_z + along_b * along_b)
    mixed_real = spec_real
    mixed_imag = spec_imag
    for term in range(TERMS):
        weight = jnp.exp(-chi_width[term] * ksquare)
        mixed_real = mixed_real + jnp.einsum('ab,bxyz->axyz', chi_amp[term], weight * spec_real, precision=lax.Precision.HIGHEST)
        mixed_imag = mixed_imag + jnp.einsum('ab,bxyz->axyz', chi_amp[term], weight * spec_imag, precision=lax.Precision.HIGHEST)
    total_corr = jnp.fft.irfftn(lax.complex(mixed_real, mixed_imag), s=(NA, NZ, NB), axes=(1, 2, 3)).astype(correlation.dtype)
    indirect = total_corr - correlation
    onehot = (species[:, None] == jnp.arange(SPECIES).astype(jnp.int32)[None, :]).astype(correlation.dtype)
    energy = jnp.einsum('sk,kxyz->sxyz', onehot, lj_field, precision=lax.Precision.HIGHEST)
    energy = energy + charges.astype(correlation.dtype)[:, None, None, None] * potential[None]
    shifted = indirect - energy
    next_corr = jnp.where(shifted < 0, jnp.expm1(jnp.minimum(shifted, 0.0)), shifted) - indirect
    change = next_corr - correlation
    residual_rms = jnp.sqrt(jnp.sum(change * change) / (SITES * NA * NZ * NB) + 1e-06).reshape(1)
    return (total_corr, next_corr, residual_rms)
```

```python
import math

import jax
import jax.numpy as jnp
import ml_dtypes
import numpy as np
from jax import lax
from jax.experimental import pallas as pl
from jax.experimental.pallas import tpu as pltpu
from jax.sharding import PartitionSpec as P

full_turn = 2.0 * math.pi
precise = lax.Precision.HIGHEST
f32 = jnp.float32
bf16 = jnp.bfloat16


def hartley(n):
    product = np.outer(np.arange(n), np.arange(n)) % n
    theta = product * (full_turn / n)
    return (np.cos(theta) + np.sin(theta)) / math.sqrt(n)


def halves(matrix):
    high = matrix.astype(ml_dtypes.bfloat16)
    low = (matrix - high.astype(np.float64)).astype(ml_dtypes.bfloat16)
    return jnp.asarray(np.stack((high, low)))


def signed_square(n):
    index = np.arange(n)
    freq = ((index + n // 2) % n - n // 2) / n
    return (full_turn * full_turn * freq * freq).astype(np.float32)


def split(values):
    high = values.astype(bf16)
    return high, (values - high.astype(f32)).astype(bf16)


def mul(left, right):
    return jnp.dot(left, right, preferred_element_type=f32)


def left_by(table, values):
    high, low = split(values)
    return mul(table[0], high) + (mul(table[0], low) + mul(table[1], high))


def right_by(values, table):
    high, low = split(values)
    return mul(high, table[0]) + (mul(low, table[0]) + mul(high, table[1]))


def head_kernel(x_ref, b_ref, z_ref, *outs):
    rows, depth, columns = x_ref.shape[1:]
    devices = outs[0].shape[0]
    group = z_ref.shape[1] // depth
    for i in range(rows // group):
        part = x_ref[0, i * group:(i + 1) * group].reshape(group * depth, columns)
        turned = left_by(z_ref, right_by(part, b_ref)).reshape(depth, group, columns)
        for j, out in enumerate(outs):
            out[:, 0, i * group:(i + 1) * group, :] = turned[j * devices:(j + 1) * devices]


def middle_kernel(amp_ref, width_ref, kz_ref, x_ref, a_ref, ka_ref, kb_ref, out_ref, work_ref):
    devices, sites, rows, columns = x_ref.shape
    terms = width_ref.shape[0]
    extent = devices * rows
    for s in range(sites):
        work_ref[s] = left_by(a_ref, x_ref[:, s].reshape(extent, columns))

    @pl.loop(0, extent // 8)
    def _(step):
        here = pl.ds(pl.multiple_of(step * 8, 8), 8)
        square = ka_ref[here, :] + kb_ref[...] + kz_ref[0]
        weights = [jnp.exp(-width_ref[m] * square) for m in range(terms)]
        values = [work_ref[t, here, :] for t in range(sites)]
        for s in range(sites):
            total = values[s]
            for t in range(sites):
                factor = amp_ref[s * sites + t] * weights[0]
                for m in range(1, terms):
                    factor = factor + amp_ref[(m * sites + s) * sites + t] * weights[m]
                total = total + factor * values[t]
            work_ref[s, here, :] = total

    for s in range(sites):
        out_ref[:, s] = left_by(a_ref, work_ref[s]).reshape(devices, rows, columns)


def tail_kernel(species_ref, charge_ref, *refs):
    count = len(refs) - 8
    parts = refs[:count]
    x_ref, lj_ref, pot_ref, b_ref, z_ref, total_ref, next_ref, sum_ref = refs[count:]
    site = pl.program_id(0)
    rows, depth, columns = x_ref.shape[1:]
    devices = parts[0].shape[0]
    group = z_ref.shape[1] // depth

    @pl.when(site == 0)
    def _():
        sum_ref[...] = jnp.zeros_like(sum_ref)

    charge = charge_ref[site]
    for i in range(rows // group):
        here = slice(i * group, (i + 1) * group)
        blocks = [part[:, 0, here, :].reshape(devices * group, columns) for part in parts]
        joined = jnp.concatenate(blocks, axis=0) if count > 1 else blocks[0]
        total = right_by(left_by(z_ref, joined), b_ref).reshape(group, depth, columns)
        before = x_ref[0, here]
        indirect = total - before
        shifted = indirect - (lj_ref[0, here] + charge * pot_ref[here])
        after = jnp.where(shifted < 0, jnp.exp(jnp.minimum(shifted, 0.0)) - 1.0, shifted) - indirect
        change = after - before
        total_ref[0, here] = total
        next_ref[0, here] = after
        sum_ref[...] += jnp.sum((change * change).reshape(-1, 8, columns), axis=0)


def plain_mix(values, square, chi_amp, chi_width):
    weight = jnp.exp(-chi_width.reshape((-1,) + (1,) * square.ndim) * square[None])
    scaled = weight[:, None] * values[None]
    return values + jnp.einsum("mab,mb...->a...", chi_amp, scaled, precision=precise)


def convolved_plain(x, chi_amp, chi_width, me, devices):
    sites, rows, depth, columns = x.shape
    extent = rows * devices
    b_table = jnp.asarray(hartley(columns), f32)
    z_table = jnp.asarray(hartley(depth), f32)
    a_table = jnp.asarray(hartley(extent), f32)
    y = jnp.einsum("sazb,bk->sazk", x, b_table, precision=precise)
    y = jnp.einsum("sazk,zl->salk", y, z_table, precision=precise)
    share = depth * columns // devices
    y = y.reshape(sites, rows, devices, share).transpose(2, 0, 1, 3)
    y = lax.all_to_all(y, "slab", split_axis=0, concat_axis=0)
    y = jnp.einsum("dsrc,drk->skc", y, a_table.reshape(devices, rows, extent), precision=precise)
    plane = (signed_square(depth)[:, None] + signed_square(columns)[None, :]).reshape(devices, share)
    mine = lax.dynamic_index_in_dim(jnp.asarray(plane), me, 0, keepdims=False)
    square = jnp.asarray(signed_square(extent))[:, None] + mine[None, :]
    y = plain_mix(y, square, chi_amp, chi_width)
    y = jnp.einsum("skc,drk->dsrc", y, a_table.reshape(devices, rows, extent), precision=precise)
    y = lax.all_to_all(y, "slab", split_axis=0, concat_axis=0)
    y = y.transpose(1, 2, 0, 3).reshape(sites, rows, depth, columns)
    y = jnp.einsum("salk,zl->sazk", y, z_table, precision=precise)
    return jnp.einsum("sazk,bk->sazb", y, b_table, precision=precise)


def closure_plain(total_corr, correlation, lj_field, potential, species, charges):
    indirect = total_corr - correlation
    energy = lj_field[species] + charges.astype(f32)[:, None, None, None] * potential[None]
    shifted = indirect - energy
    next_corr = jnp.where(shifted < 0, jnp.expm1(jnp.minimum(shifted, 0.0)), shifted) - indirect
    change = next_corr - correlation
    return next_corr, change * change


vmem = pl.BlockSpec(memory_space=pltpu.VMEM)
smem = pl.BlockSpec(memory_space=pltpu.SMEM)
limit = 56 * 1024 * 1024


def body(correlation, lj_field, potential, species, charges, chi_amp, chi_width):
    sites, rows, depth, columns = correlation.shape
    devices = lax.axis_size("slab")
    me = lax.axis_index("slab")
    extent = rows * devices
    cells = sites * extent * depth * columns

    if depth % devices or rows % 8 or columns % 128:
        total_corr = convolved_plain(correlation, chi_amp, chi_width, me, devices)
        next_corr, squares = closure_plain(
            total_corr, correlation, lj_field, potential, species, charges
        )
        summed = lax.psum(jnp.sum(squares), "slab")
        return (total_corr, next_corr, jnp.sqrt(summed / cells + 1e-06).reshape(1))

    group = 8
    chunks = depth // devices
    z_basis = hartley(depth)
    forward = np.einsum("kz,ab->kabz", z_basis, np.eye(group)).reshape(group * depth, group * depth)
    b_table = halves(hartley(columns))
    a_table = halves(hartley(extent))
    z_table = halves(forward)
    z_back = halves(forward.T)
    b_spec = pl.BlockSpec((2, columns, columns), lambda s, *_: (0, 0, 0))
    z_spec = pl.BlockSpec((2, group * depth, group * depth), lambda s, *_: (0, 0, 0))
    row_spec = pl.BlockSpec((1, rows, depth, columns), lambda s, *_: (s, 0, 0, 0))
    part_spec = pl.BlockSpec((devices, 1, rows, columns), lambda s, *_: (0, s, 0, 0))
    part_shape = jax.ShapeDtypeStruct((devices, sites, rows, columns), f32)
    size = correlation.size

    sent = pl.pallas_call(
        head_kernel,
        grid=(sites,),
        in_specs=[row_spec, b_spec, z_spec],
        out_specs=[part_spec] * chunks,
        out_shape=[part_shape] * chunks,
        compiler_params=pltpu.CompilerParams(vmem_limit_bytes=limit),
        cost_estimate=pl.CostEstimate(
            flops=12 * size * columns, bytes_accessed=8 * size, transcendentals=0
        ),
        name="head",
    )(correlation, b_table, z_table)

    kz = jnp.asarray(signed_square(depth))
    ka = jnp.asarray(np.repeat(signed_square(extent)[:, None], columns, axis=1))
    kb = jnp.asarray(np.repeat(signed_square(columns)[None, :], 8, axis=0))
    amp = chi_amp.reshape(-1)
    arrived = []
    for j in range(chunks):
        got = lax.all_to_all(sent[j], "slab", split_axis=0, concat_axis=0, tiled=True)
        mixed = pl.pallas_call(
            middle_kernel,
            in_specs=[smem, smem, smem, vmem, vmem, vmem, vmem],
            out_specs=vmem,
            out_shape=part_shape,
            scratch_shapes=[pltpu.VMEM((sites, extent, columns), f32)],
            compiler_params=pltpu.CompilerParams(vmem_limit_bytes=limit),
            cost_estimate=pl.CostEstimate(
                flops=20 * size * extent // chunks, bytes_accessed=8 * size // chunks, transcendentals=0
            ),
            name="middle",
        )(amp, chi_width, lax.dynamic_slice(kz, (j * devices + me,), (1,)), got, a_table, ka, kb)
        arrived.append(lax.all_to_all(mixed, "slab", split_axis=0, concat_axis=0, tiled=True))

    total_corr, next_corr, sums = pl.pallas_call(
        tail_kernel,
        grid_spec=pltpu.PrefetchScalarGridSpec(
            num_scalar_prefetch=2,
            grid=(sites,),
            in_specs=[part_spec] * chunks + [
                row_spec,
                pl.BlockSpec((1, rows, depth, columns), lambda s, kind, _: (kind[s], 0, 0, 0)),
                pl.BlockSpec((rows, depth, columns), lambda s, *_: (0, 0, 0)),
                b_spec,
                z_spec,
            ],
            out_specs=[row_spec, row_spec, pl.BlockSpec((8, columns), lambda s, *_: (0, 0))],
        ),
        out_shape=[
            jax.ShapeDtypeStruct(correlation.shape, f32),
            jax.ShapeDtypeStruct(correlation.shape, f32),
            jax.ShapeDtypeStruct((8, columns), f32),
        ],
        compiler_params=pltpu.CompilerParams(vmem_limit_bytes=limit),
        cost_estimate=pl.CostEstimate(
            flops=12 * size * columns, bytes_accessed=20 * size, transcendentals=size
        ),
        name="tail",
    )(species, charges.astype(f32), *arrived, correlation, lj_field, potential, b_table, z_back)
    summed = lax.psum(jnp.sum(sums), "slab")
    return (total_corr, next_corr, jnp.sqrt(summed / cells + 1e-06).reshape(1))


def solution(mesh):
    placed = (
        P("sys", "slab", None, None),
        P("sys", "slab", None, None),
        P(("sys", "slab"), None, None),
        P(),
        P(),
        P(),
        P(),
    )
    return jax.shard_map(
        body,
        mesh=mesh,
        in_specs=placed,
        out_specs=(P("sys", "slab", None, None), P("sys", "slab", None, None), P("sys")),
        check_vma=False,
    )
```

```python
import math

import jax
import jax.numpy as jnp
import ml_dtypes
import numpy as np
from jax import lax
from jax.experimental import pallas as pl
from jax.experimental.pallas import tpu as pltpu
from jax.sharding import PartitionSpec as P

full_turn = 2.0 * math.pi
precise = lax.Precision.HIGHEST
f32 = jnp.float32
bf16 = jnp.bfloat16


def hartley(n):
    product = np.outer(np.arange(n), np.arange(n)) % n
    theta = product * (full_turn / n)
    return (np.cos(theta) + np.sin(theta)) / math.sqrt(n)


def halves(matrix):
    high = matrix.astype(ml_dtypes.bfloat16)
    low = (matrix - high.astype(np.float64)).astype(ml_dtypes.bfloat16)
    return jnp.asarray(np.stack((high, low)))


def signed_square(n):
    index = np.arange(n)
    freq = ((index + n // 2) % n - n // 2) / n
    return (full_turn * full_turn * freq * freq).astype(np.float32)


def split(values):
    high = values.astype(bf16)
    return high, (values - high.astype(f32)).astype(bf16)


def mul(left, right):
    return jnp.dot(left, right, preferred_element_type=f32)


def left_by(table, values):
    high, low = split(values)
    return mul(table[0], high) + (mul(table[0], low) + mul(table[1], high))


def right_by(values, table):
    high, low = split(values)
    return mul(high, table[0]) + (mul(low, table[0]) + mul(high, table[1]))


def head_kernel(x_ref, b_ref, z_ref, *outs):
    rows, depth, columns = x_ref.shape[1:]
    devices = outs[0].shape[0]
    group = z_ref.shape[1] // depth
    for i in range(rows // group):
        part = x_ref[0, i * group:(i + 1) * group].reshape(group * depth, columns)
        turned = left_by(z_ref, right_by(part, b_ref)).reshape(depth, group, columns)
        for j, out in enumerate(outs):
            out[:, 0, i * group:(i + 1) * group, :] = turned[j * devices:(j + 1) * devices]


def middle_kernel(amp_ref, width_ref, kz_ref, x_ref, a_ref, ka_ref, kb_ref, out_ref, work_ref):
    devices, sites, rows, columns = x_ref.shape
    terms = width_ref.shape[0]
    extent = devices * rows
    for s in range(sites):
        work_ref[s] = left_by(a_ref, x_ref[:, s].reshape(extent, columns))

    @pl.loop(0, extent // 8)
    def _(step):
        here = pl.ds(pl.multiple_of(step * 8, 8), 8)
        square = ka_ref[here, :] + kb_ref[...] + kz_ref[0]
        weights = [jnp.exp(-width_ref[m] * square) for m in range(terms)]
        values = [work_ref[t, here, :] for t in range(sites)]
        for s in range(sites):
            total = values[s]
            for t in range(sites):
                factor = amp_ref[s * sites + t] * weights[0]
                for m in range(1, terms):
                    factor = factor + amp_ref[(m * sites + s) * sites + t] * weights[m]
                total = total + factor * values[t]
            work_ref[s, here, :] = total

    for s in range(sites):
        out_ref[:, s] = left_by(a_ref, work_ref[s]).reshape(devices, rows, columns)


def tail_kernel(species_ref, charge_ref, *refs):
    count = len(refs) - 8
    parts = refs[:count]
    x_ref, lj_ref, pot_ref, b_ref, z_ref, total_ref, next_ref, sum_ref = refs[count:]
    site = pl.program_id(0)
    rows, depth, columns = x_ref.shape[1:]
    devices = parts[0].shape[0]
    group = z_ref.shape[1] // depth

    @pl.when(site == 0)
    def _():
        sum_ref[...] = jnp.zeros_like(sum_ref)

    charge = charge_ref[site]
    for i in range(rows // group):
        here = slice(i * group, (i + 1) * group)
        blocks = [part[:, 0, here, :].reshape(devices * group, columns) for part in parts]
        joined = jnp.concatenate(blocks, axis=0) if count > 1 else blocks[0]
        total = right_by(left_by(z_ref, joined), b_ref).reshape(group, depth, columns)
        before = x_ref[0, here]
        indirect = total - before
        shifted = indirect - (lj_ref[0, here] + charge * pot_ref[here])
        after = jnp.where(shifted < 0, jnp.exp(jnp.minimum(shifted, 0.0)) - 1.0, shifted) - indirect
        change = after - before
        total_ref[0, here] = total
        next_ref[0, here] = after
        sum_ref[...] += jnp.sum((change * change).reshape(-1, 8, columns), axis=0)


def gather_kernel(sum_ref, out_ref, mine_ref, slots_ref, send_sem, recv_sem):
    devices = slots_ref.shape[0]
    me = lax.axis_index("slab")
    barrier = pltpu.get_barrier_semaphore()
    for i in range(1, devices):
        pl.semaphore_signal(barrier, inc=1, device_id={"slab": lax.rem(me + i, devices)})
    total = sum_ref[:, :128]
    for i in range(1, sum_ref.shape[1] // 128):
        total = total + sum_ref[:, i * 128:(i + 1) * 128]
    mine_ref[...] = total
    slots_ref[me] = total
    pl.semaphore_wait(barrier, devices - 1)
    copies = []
    for i in range(1, devices):
        copy = pltpu.make_async_remote_copy(
            src_ref=mine_ref,
            dst_ref=slots_ref.at[me],
            send_sem=send_sem.at[i],
            recv_sem=recv_sem.at[i],
            device_id={"slab": lax.rem(me + i, devices)},
        )
        copy.start()
        copies.append(copy)
    for copy in copies:
        copy.wait()
    out_ref[...] = jnp.sum(slots_ref[...], axis=0)


def plain_mix(values, square, chi_amp, chi_width):
    weight = jnp.exp(-chi_width.reshape((-1,) + (1,) * square.ndim) * square[None])
    scaled = weight[:, None] * values[None]
    return values + jnp.einsum("mab,mb...->a...", chi_amp, scaled, precision=precise)


def convolved_plain(x, chi_amp, chi_width, me, devices):
    sites, rows, depth, columns = x.shape
    extent = rows * devices
    b_table = jnp.asarray(hartley(columns), f32)
    z_table = jnp.asarray(hartley(depth), f32)
    a_table = jnp.asarray(hartley(extent), f32)
    y = jnp.einsum("sazb,bk->sazk", x, b_table, precision=precise)
    y = jnp.einsum("sazk,zl->salk", y, z_table, precision=precise)
    share = depth * columns // devices
    y = y.reshape(sites, rows, devices, share).transpose(2, 0, 1, 3)
    y = lax.all_to_all(y, "slab", split_axis=0, concat_axis=0)
    y = jnp.einsum("dsrc,drk->skc", y, a_table.reshape(devices, rows, extent), precision=precise)
    plane = (signed_square(depth)[:, None] + signed_square(columns)[None, :]).reshape(devices, share)
    mine = lax.dynamic_index_in_dim(jnp.asarray(plane), me, 0, keepdims=False)
    square = jnp.asarray(signed_square(extent))[:, None] + mine[None, :]
    y = plain_mix(y, square, chi_amp, chi_width)
    y = jnp.einsum("skc,drk->dsrc", y, a_table.reshape(devices, rows, extent), precision=precise)
    y = lax.all_to_all(y, "slab", split_axis=0, concat_axis=0)
    y = y.transpose(1, 2, 0, 3).reshape(sites, rows, depth, columns)
    y = jnp.einsum("salk,zl->sazk", y, z_table, precision=precise)
    return jnp.einsum("sazk,bk->sazb", y, b_table, precision=precise)


def closure_plain(total_corr, correlation, lj_field, potential, species, charges):
    indirect = total_corr - correlation
    energy = lj_field[species] + charges.astype(f32)[:, None, None, None] * potential[None]
    shifted = indirect - energy
    next_corr = jnp.where(shifted < 0, jnp.expm1(jnp.minimum(shifted, 0.0)), shifted) - indirect
    change = next_corr - correlation
    return next_corr, change * change


vmem = pl.BlockSpec(memory_space=pltpu.VMEM)
smem = pl.BlockSpec(memory_space=pltpu.SMEM)
limit = 56 * 1024 * 1024


def body(correlation, lj_field, potential, species, charges, chi_amp, chi_width):
    sites, rows, depth, columns = correlation.shape
    devices = lax.axis_size("slab")
    me = lax.axis_index("slab")
    extent = rows * devices
    cells = sites * extent * depth * columns

    if depth % devices or rows % 8 or columns % 128:
        total_corr = convolved_plain(correlation, chi_amp, chi_width, me, devices)
        next_corr, squares = closure_plain(
            total_corr, correlation, lj_field, potential, species, charges
        )
        summed = lax.psum(jnp.sum(squares), "slab")
        return (total_corr, next_corr, jnp.sqrt(summed / cells + 1e-06).reshape(1))

    group = 8
    chunks = depth // devices
    z_basis = hartley(depth)
    forward = np.einsum("kz,ab->kabz", z_basis, np.eye(group)).reshape(group * depth, group * depth)
    b_table = halves(hartley(columns))
    a_table = halves(hartley(extent))
    z_table = halves(forward)
    z_back = halves(forward.T)
    b_spec = pl.BlockSpec((2, columns, columns), lambda s, *_: (0, 0, 0))
    z_spec = pl.BlockSpec((2, group * depth, group * depth), lambda s, *_: (0, 0, 0))
    row_spec = pl.BlockSpec((1, rows, depth, columns), lambda s, *_: (s, 0, 0, 0))
    part_spec = pl.BlockSpec((devices, 1, rows, columns), lambda s, *_: (0, s, 0, 0))
    part_shape = jax.ShapeDtypeStruct((devices, sites, rows, columns), f32)
    size = correlation.size

    sent = pl.pallas_call(
        head_kernel,
        grid=(sites,),
        in_specs=[row_spec, b_spec, z_spec],
        out_specs=[part_spec] * chunks,
        out_shape=[part_shape] * chunks,
        compiler_params=pltpu.CompilerParams(vmem_limit_bytes=limit),
        cost_estimate=pl.CostEstimate(
            flops=12 * size * columns, bytes_accessed=8 * size, transcendentals=0
        ),
        name="head",
    )(correlation, b_table, z_table)

    kz = jnp.asarray(signed_square(depth))
    ka = jnp.asarray(np.repeat(signed_square(extent)[:, None], columns, axis=1))
    kb = jnp.asarray(np.repeat(signed_square(columns)[None, :], 8, axis=0))
    amp = chi_amp.reshape(-1)
    arrived = []
    for j in range(chunks):
        got = lax.all_to_all(sent[j], "slab", split_axis=0, concat_axis=0, tiled=True)
        mixed = pl.pallas_call(
            middle_kernel,
            in_specs=[smem, smem, smem, vmem, vmem, vmem, vmem],
            out_specs=vmem,
            out_shape=part_shape,
            scratch_shapes=[pltpu.VMEM((sites, extent, columns), f32)],
            compiler_params=pltpu.CompilerParams(vmem_limit_bytes=limit),
            cost_estimate=pl.CostEstimate(
                flops=20 * size * extent // chunks, bytes_accessed=8 * size // chunks, transcendentals=0
            ),
            name="middle",
        )(amp, chi_width, lax.dynamic_slice(kz, (j * devices + me,), (1,)), got, a_table, ka, kb)
        arrived.append(lax.all_to_all(mixed, "slab", split_axis=0, concat_axis=0, tiled=True))

    total_corr, next_corr, sums = pl.pallas_call(
        tail_kernel,
        grid_spec=pltpu.PrefetchScalarGridSpec(
            num_scalar_prefetch=2,
            grid=(sites,),
            in_specs=[part_spec] * chunks + [
                row_spec,
                pl.BlockSpec((1, rows, depth, columns), lambda s, kind, _: (kind[s], 0, 0, 0)),
                pl.BlockSpec((rows, depth, columns), lambda s, *_: (0, 0, 0)),
                b_spec,
                z_spec,
            ],
            out_specs=[row_spec, row_spec, pl.BlockSpec((8, columns), lambda s, *_: (0, 0))],
        ),
        out_shape=[
            jax.ShapeDtypeStruct(correlation.shape, f32),
            jax.ShapeDtypeStruct(correlation.shape, f32),
            jax.ShapeDtypeStruct((8, columns), f32),
        ],
        compiler_params=pltpu.CompilerParams(vmem_limit_bytes=limit),
        cost_estimate=pl.CostEstimate(
            flops=12 * size * columns, bytes_accessed=20 * size, transcendentals=size
        ),
        name="tail",
    )(species, charges.astype(f32), *arrived, correlation, lj_field, potential, b_table, z_back)
    gathered = pl.pallas_call(
        gather_kernel,
        in_specs=[vmem],
        out_specs=vmem,
        out_shape=jax.ShapeDtypeStruct((8, 128), f32),
        scratch_shapes=[
            pltpu.VMEM((8, 128), f32),
            pltpu.VMEM((devices, 8, 128), f32),
            pltpu.SemaphoreType.DMA((devices,)),
            pltpu.SemaphoreType.DMA((devices,)),
        ],
        compiler_params=pltpu.CompilerParams(collective_id=0, has_side_effects=True),
        name="gather",
    )(sums)
    summed = jnp.sum(gathered)
    return (total_corr, next_corr, jnp.sqrt(summed / cells + 1e-06).reshape(1))


def solution(mesh):
    placed = (
        P("sys", "slab", None, None),
        P("sys", "slab", None, None),
        P(("sys", "slab"), None, None),
        P(),
        P(),
        P(),
        P(),
    )
    return jax.shard_map(
        body,
        mesh=mesh,
        in_specs=placed,
        out_specs=(P("sys", "slab", None, None), P("sys", "slab", None, None), P("sys")),
        check_vma=False,
    )
```

```python
import math

import jax
import jax.numpy as jnp
import ml_dtypes
import numpy as np
from jax import lax
from jax.experimental import pallas as pl
from jax.experimental.pallas import tpu as pltpu
from jax.sharding import PartitionSpec as P

full_turn = 2.0 * math.pi
precise = lax.Precision.HIGHEST
f32 = jnp.float32
bf16 = jnp.bfloat16


def hartley(n):
    product = np.outer(np.arange(n), np.arange(n)) % n
    theta = product * (full_turn / n)
    return (np.cos(theta) + np.sin(theta)) / math.sqrt(n)


def halves(matrix):
    high = matrix.astype(ml_dtypes.bfloat16)
    low = (matrix - high.astype(np.float64)).astype(ml_dtypes.bfloat16)
    return jnp.asarray(np.stack((high, low)))


def signed_square(n):
    index = np.arange(n)
    freq = ((index + n // 2) % n - n // 2) / n
    return (full_turn * full_turn * freq * freq).astype(np.float32)


def split(values):
    high = values.astype(bf16)
    return high, (values - high.astype(f32)).astype(bf16)


def mul(left, right):
    return jnp.dot(left, right, preferred_element_type=f32)


def left_by(table, values):
    high, low = split(values)
    return mul(table[0], high) + (mul(table[0], low) + mul(table[1], high))


def right_by(values, table):
    high, low = split(values)
    return mul(high, table[0]) + (mul(low, table[0]) + mul(high, table[1]))


def core_kernel(
    amp_ref, width_ref, kz_ref, x_ref, b_ref, z_ref, a_ref, ka_ref, kb_ref, out_ref,
    sent_ref, got_ref, work_ref, back_ref, send_sem, recv_sem, back_send, back_recv, own_sem,
):
    sites, rows, depth, columns = x_ref.shape
    chunks, devices = sent_ref.shape[:2]
    terms = width_ref.shape[0]
    extent = devices * rows
    group = z_ref.shape[1] // depth
    batches = send_sem.shape[1]
    batch = sites // batches
    me = lax.axis_index("slab")

    def spread(j, g, i):
        peer = lax.rem(me + i, devices)
        own = pl.ds(g * batch, batch)
        return pltpu.make_async_remote_copy(
            src_ref=sent_ref.at[j, peer, own],
            dst_ref=got_ref.at[j, me, own],
            send_sem=send_sem.at[j, g, i],
            recv_sem=recv_sem.at[j, g, i],
            device_id={"slab": peer},
        )

    def restore(j, g, i):
        peer = lax.rem(me + i, devices)
        own = pl.ds(g * batch, batch)
        return pltpu.make_async_remote_copy(
            src_ref=back_ref.at[j, peer, own],
            dst_ref=out_ref.at[j, me, own],
            send_sem=back_send.at[j, g, i],
            recv_sem=back_recv.at[j, g, i],
            device_id={"slab": peer},
        )

    def keep(j):
        return pltpu.make_async_copy(back_ref.at[j, me], out_ref.at[j, me], own_sem.at[j])

    barrier = pltpu.get_barrier_semaphore()

    @pl.loop(1, devices)
    def _(i):
        pl.semaphore_signal(barrier, inc=1, device_id={"slab": lax.rem(me + i, devices)})

    pl.semaphore_wait(barrier, devices - 1)

    @pl.loop(0, batches)
    def _(g):
        for k in range(batch):
            s = g * batch + k
            for r in range(rows // group):
                here = slice(r * group, (r + 1) * group)
                part = x_ref[s, here].reshape(group * depth, columns)
                turned = left_by(z_ref, right_by(part, b_ref)).reshape(depth, group, columns)
                for j in range(chunks):
                    sent_ref[j, :, s, here, :] = turned[j * devices:(j + 1) * devices]

        @pl.loop(1, devices)
        def _(i):
            spread(0, g, i).start()

    @pl.loop(1, chunks)
    def _(j):
        @pl.loop(0, batches)
        def _(g):
            @pl.loop(1, devices)
            def _(i):
                spread(j, g, i).start()

    @pl.loop(0, chunks)
    def _(j):
        got_ref[j, me] = sent_ref[j, me]

        @pl.loop(0, batches)
        def _(g):
            @pl.loop(1, devices)
            def _(i):
                spread(j, g, i).wait_recv()

            for k in range(batch):
                s = g * batch + k
                work_ref[s] = left_by(a_ref, got_ref[j, :, s].reshape(extent, columns))

        @pl.loop(0, extent // 8)
        def _(step):
            here = pl.ds(pl.multiple_of(step * 8, 8), 8)
            square = ka_ref[here, :] + kb_ref[...] + kz_ref[j * devices + me]
            weights = [jnp.exp(-width_ref[m] * square) for m in range(terms)]
            values = [work_ref[t, here, :] for t in range(sites)]
            for s in range(sites):
                total = values[s]
                for t in range(sites):
                    factor = amp_ref[s * sites + t] * weights[0]
                    for m in range(1, terms):
                        factor = factor + amp_ref[(m * sites + s) * sites + t] * weights[m]
                    total = total + factor * values[t]
                work_ref[s, here, :] = total

        @pl.loop(0, batches)
        def _(g):
            for k in range(batch):
                s = g * batch + k
                back_ref[j, :, s] = left_by(a_ref, work_ref[s]).reshape(devices, rows, columns)

            @pl.loop(1, devices)
            def _(i):
                restore(j, g, i).start()

        keep(j).start()

    @pl.loop(0, chunks)
    def _(j):
        keep(j).wait()

        @pl.loop(0, batches)
        def _(g):
            @pl.loop(1, devices)
            def _(i):
                spread(j, g, i).wait_send()
                restore(j, g, i).wait()


def tail_kernel(species_ref, charge_ref, *refs):
    parts_ref, x_ref, lj_ref, pot_ref, b_ref, z_ref, total_ref, next_ref, sum_ref = refs
    site = pl.program_id(0)
    rows, depth, columns = x_ref.shape[1:]
    chunks, devices = parts_ref.shape[:2]
    group = z_ref.shape[1] // depth

    @pl.when(site == 0)
    def _():
        sum_ref[...] = jnp.zeros_like(sum_ref)

    charge = charge_ref[site]
    for i in range(rows // group):
        here = slice(i * group, (i + 1) * group)
        joined = parts_ref[:, :, 0, here, :].reshape(chunks * devices * group, columns)
        total = right_by(left_by(z_ref, joined), b_ref).reshape(group, depth, columns)
        before = x_ref[0, here]
        indirect = total - before
        shifted = indirect - (lj_ref[0, here] + charge * pot_ref[here])
        after = jnp.where(shifted < 0, jnp.exp(jnp.minimum(shifted, 0.0)) - 1.0, shifted) - indirect
        change = after - before
        total_ref[0, here] = total
        next_ref[0, here] = after
        sum_ref[...] += jnp.sum((change * change).reshape(-1, 8, columns), axis=0)


def gather_kernel(sum_ref, out_ref, mine_ref, slots_ref, send_sem, recv_sem):
    devices = slots_ref.shape[0]
    me = lax.axis_index("slab")
    barrier = pltpu.get_barrier_semaphore()
    for i in range(1, devices):
        pl.semaphore_signal(barrier, inc=1, device_id={"slab": lax.rem(me + i, devices)})
    total = sum_ref[:, :128]
    for i in range(1, sum_ref.shape[1] // 128):
        total = total + sum_ref[:, i * 128:(i + 1) * 128]
    mine_ref[...] = total
    slots_ref[me] = total
    pl.semaphore_wait(barrier, devices - 1)
    copies = []
    for i in range(1, devices):
        copy = pltpu.make_async_remote_copy(
            src_ref=mine_ref,
            dst_ref=slots_ref.at[me],
            send_sem=send_sem.at[i],
            recv_sem=recv_sem.at[i],
            device_id={"slab": lax.rem(me + i, devices)},
        )
        copy.start()
        copies.append(copy)
    for copy in copies:
        copy.wait()
    out_ref[...] = jnp.sum(slots_ref[...], axis=0)


def plain_mix(values, square, chi_amp, chi_width):
    weight = jnp.exp(-chi_width.reshape((-1,) + (1,) * square.ndim) * square[None])
    scaled = weight[:, None] * values[None]
    return values + jnp.einsum("mab,mb...->a...", chi_amp, scaled, precision=precise)


def convolved_plain(x, chi_amp, chi_width, me, devices):
    sites, rows, depth, columns = x.shape
    extent = rows * devices
    b_table = jnp.asarray(hartley(columns), f32)
    z_table = jnp.asarray(hartley(depth), f32)
    a_table = jnp.asarray(hartley(extent), f32)
    y = jnp.einsum("sazb,bk->sazk", x, b_table, precision=precise)
    y = jnp.einsum("sazk,zl->salk", y, z_table, precision=precise)
    share = depth * columns // devices
    y = y.reshape(sites, rows, devices, share).transpose(2, 0, 1, 3)
    y = lax.all_to_all(y, "slab", split_axis=0, concat_axis=0)
    y = jnp.einsum("dsrc,drk->skc", y, a_table.reshape(devices, rows, extent), precision=precise)
    plane = (signed_square(depth)[:, None] + signed_square(columns)[None, :]).reshape(devices, share)
    mine = lax.dynamic_index_in_dim(jnp.asarray(plane), me, 0, keepdims=False)
    square = jnp.asarray(signed_square(extent))[:, None] + mine[None, :]
    y = plain_mix(y, square, chi_amp, chi_width)
    y = jnp.einsum("skc,drk->dsrc", y, a_table.reshape(devices, rows, extent), precision=precise)
    y = lax.all_to_all(y, "slab", split_axis=0, concat_axis=0)
    y = y.transpose(1, 2, 0, 3).reshape(sites, rows, depth, columns)
    y = jnp.einsum("salk,zl->sazk", y, z_table, precision=precise)
    return jnp.einsum("sazk,bk->sazb", y, b_table, precision=precise)


def closure_plain(total_corr, correlation, lj_field, potential, species, charges):
    indirect = total_corr - correlation
    energy = lj_field[species] + charges.astype(f32)[:, None, None, None] * potential[None]
    shifted = indirect - energy
    next_corr = jnp.where(shifted < 0, jnp.expm1(jnp.minimum(shifted, 0.0)), shifted) - indirect
    change = next_corr - correlation
    return next_corr, change * change


vmem = pl.BlockSpec(memory_space=pltpu.VMEM)
smem = pl.BlockSpec(memory_space=pltpu.SMEM)
limit = 56 * 1024 * 1024


def body(correlation, lj_field, potential, species, charges, chi_amp, chi_width):
    sites, rows, depth, columns = correlation.shape
    devices = lax.axis_size("slab")
    me = lax.axis_index("slab")
    extent = rows * devices
    cells = sites * extent * depth * columns

    if depth % devices or rows % 8 or columns % 128:
        total_corr = convolved_plain(correlation, chi_amp, chi_width, me, devices)
        next_corr, squares = closure_plain(
            total_corr, correlation, lj_field, potential, species, charges
        )
        summed = lax.psum(jnp.sum(squares), "slab")
        return (total_corr, next_corr, jnp.sqrt(summed / cells + 1e-06).reshape(1))

    group = 8
    chunks = depth // devices
    z_basis = hartley(depth)
    forward = np.einsum("kz,ab->kabz", z_basis, np.eye(group)).reshape(group * depth, group * depth)
    b_table = halves(hartley(columns))
    a_table = halves(hartley(extent))
    z_table = halves(forward)
    z_back = halves(forward.T)
    b_spec = pl.BlockSpec((2, columns, columns), lambda s, *_: (0, 0, 0))
    z_spec = pl.BlockSpec((2, group * depth, group * depth), lambda s, *_: (0, 0, 0))
    row_spec = pl.BlockSpec((1, rows, depth, columns), lambda s, *_: (s, 0, 0, 0))
    part_spec = pl.BlockSpec(
        (chunks, devices, 1, rows, columns), lambda s, *_: (0, 0, s, 0, 0)
    )
    whole = (chunks, devices, sites, rows, columns)
    size = correlation.size
    batches = 4 if sites % 4 == 0 else 1
    pairs = pltpu.SemaphoreType.DMA((chunks, batches, devices))

    kz = jnp.asarray(signed_square(depth))
    ka = jnp.asarray(np.repeat(signed_square(extent)[:, None], columns, axis=1))
    kb = jnp.asarray(np.repeat(signed_square(columns)[None, :], 8, axis=0))
    arrived = pl.pallas_call(
        core_kernel,
        in_specs=[smem, smem, smem] + [vmem] * 6,
        out_specs=pl.BlockSpec(memory_space=pl.ANY),
        out_shape=jax.ShapeDtypeStruct(whole, f32),
        scratch_shapes=[
            pltpu.VMEM(whole, f32),
            pltpu.VMEM(whole, f32),
            pltpu.VMEM((sites, extent, columns), f32),
            pltpu.VMEM(whole, f32),
            pairs,
            pairs,
            pairs,
            pairs,
            pltpu.SemaphoreType.DMA((chunks,)),
        ],
        compiler_params=pltpu.CompilerParams(
            collective_id=1, has_side_effects=True, vmem_limit_bytes=limit
        ),
        name="core",
    )(chi_amp.reshape(-1), chi_width, kz, correlation, b_table, z_table, a_table, ka, kb)

    total_corr, next_corr, sums = pl.pallas_call(
        tail_kernel,
        grid_spec=pltpu.PrefetchScalarGridSpec(
            num_scalar_prefetch=2,
            grid=(sites,),
            in_specs=[
                part_spec,
                row_spec,
                pl.BlockSpec((1, rows, depth, columns), lambda s, kind, _: (kind[s], 0, 0, 0)),
                pl.BlockSpec((rows, depth, columns), lambda s, *_: (0, 0, 0)),
                b_spec,
                z_spec,
            ],
            out_specs=[row_spec, row_spec, pl.BlockSpec((8, columns), lambda s, *_: (0, 0))],
        ),
        out_shape=[
            jax.ShapeDtypeStruct(correlation.shape, f32),
            jax.ShapeDtypeStruct(correlation.shape, f32),
            jax.ShapeDtypeStruct((8, columns), f32),
        ],
        compiler_params=pltpu.CompilerParams(vmem_limit_bytes=limit),
        cost_estimate=pl.CostEstimate(
            flops=12 * size * columns, bytes_accessed=20 * size, transcendentals=size
        ),
        name="tail",
    )(species, charges.astype(f32), arrived, correlation, lj_field, potential, b_table, z_back)
    gathered = pl.pallas_call(
        gather_kernel,
        in_specs=[vmem],
        out_specs=vmem,
        out_shape=jax.ShapeDtypeStruct((8, 128), f32),
        scratch_shapes=[
            pltpu.VMEM((8, 128), f32),
            pltpu.VMEM((devices, 8, 128), f32),
            pltpu.SemaphoreType.DMA((devices,)),
            pltpu.SemaphoreType.DMA((devices,)),
        ],
        compiler_params=pltpu.CompilerParams(collective_id=0, has_side_effects=True),
        name="gather",
    )(sums)
    summed = jnp.sum(gathered)
    return (total_corr, next_corr, jnp.sqrt(summed / cells + 1e-06).reshape(1))


def solution(mesh):
    placed = (
        P("sys", "slab", None, None),
        P("sys", "slab", None, None),
        P(("sys", "slab"), None, None),
        P(),
        P(),
        P(),
        P(),
    )
    return jax.shard_map(
        body,
        mesh=mesh,
        in_specs=placed,
        out_specs=(P("sys", "slab", None, None), P("sys", "slab", None, None), P("sys")),
        check_vma=False,
    )
```

```python
import math

import jax
import jax.numpy as jnp
import ml_dtypes
import numpy as np
from jax import lax
from jax.experimental import pallas as pl
from jax.experimental.pallas import tpu as pltpu
from jax.sharding import PartitionSpec as P

full_turn = 2.0 * math.pi
precise = lax.Precision.HIGHEST
f32 = jnp.float32
bf16 = jnp.bfloat16


def hartley(n):
    product = np.outer(np.arange(n), np.arange(n)) % n
    theta = product * (full_turn / n)
    return (np.cos(theta) + np.sin(theta)) / math.sqrt(n)


def halves(matrix):
    high = matrix.astype(ml_dtypes.bfloat16)
    low = (matrix - high.astype(np.float64)).astype(ml_dtypes.bfloat16)
    return jnp.asarray(np.stack((high, low)))


def signed_square(n):
    index = np.arange(n)
    freq = ((index + n // 2) % n - n // 2) / n
    return (full_turn * full_turn * freq * freq).astype(np.float32)


def split(values):
    high = values.astype(bf16)
    return high, (values - high.astype(f32)).astype(bf16)


def mul(left, right):
    return jnp.dot(left, right, preferred_element_type=f32)


def left_by(table, values):
    high, low = split(values)
    return mul(table[0], high) + (mul(table[0], low) + mul(table[1], high))


def right_by(values, table):
    high, low = split(values)
    return mul(high, table[0]) + (mul(low, table[0]) + mul(high, table[1]))


def core_kernel(
    amp_ref, width_ref, kz_ref, x_ref, b_ref, z_ref, a_ref, ka_ref, kb_ref, out_ref,
    sent_ref, got_ref, work_ref, back_ref, send_sem, recv_sem, back_send, back_recv, own_sem,
):
    sites, rows, depth, columns = x_ref.shape
    chunks, devices = sent_ref.shape[:2]
    terms = width_ref.shape[0]
    extent = devices * rows
    group = z_ref.shape[1] // depth
    batches = send_sem.shape[1]
    batch = sites // batches
    me = lax.axis_index("slab")

    def spread(j, g, i):
        peer = lax.rem(me + 1 + lax.rem(i + devices // 2 - 2, devices - 1), devices)
        own = pl.ds(g * batch, batch)
        return pltpu.make_async_remote_copy(
            src_ref=sent_ref.at[j, peer, own],
            dst_ref=got_ref.at[j, me, own],
            send_sem=send_sem.at[j, g, i],
            recv_sem=recv_sem.at[j, g, i],
            device_id={"slab": peer},
        )

    def restore(j, g, i):
        peer = lax.rem(me + 1 + lax.rem(i + devices // 2 - 2, devices - 1), devices)
        own = pl.ds(g * batch, batch)
        return pltpu.make_async_remote_copy(
            src_ref=back_ref.at[j, peer, own],
            dst_ref=out_ref.at[j, me, own],
            send_sem=back_send.at[j, g, i],
            recv_sem=back_recv.at[j, g, i],
            device_id={"slab": peer},
        )

    def keep(j):
        return pltpu.make_async_copy(back_ref.at[j, me], out_ref.at[j, me], own_sem.at[j])

    barrier = pltpu.get_barrier_semaphore()

    @pl.loop(1, devices)
    def _(i):
        pl.semaphore_signal(barrier, inc=1, device_id={"slab": lax.rem(me + i, devices)})

    pl.semaphore_wait(barrier, devices - 1)

    @pl.loop(0, batches)
    def _(g):
        for k in range(batch):
            s = g * batch + k
            for r in range(rows // group):
                here = slice(r * group, (r + 1) * group)
                part = x_ref[s, here].reshape(group * depth, columns)
                turned = left_by(z_ref, right_by(part, b_ref)).reshape(depth, group, columns)
                for j in range(chunks):
                    sent_ref[j, :, s, here, :] = turned[j * devices:(j + 1) * devices]

        @pl.loop(1, devices)
        def _(i):
            spread(0, g, i).start()

    @pl.loop(1, chunks)
    def _(j):
        @pl.loop(0, batches)
        def _(g):
            @pl.loop(1, devices)
            def _(i):
                spread(j, g, i).start()

    @pl.loop(0, chunks)
    def _(j):
        got_ref[j, me] = sent_ref[j, me]

        @pl.loop(0, batches)
        def _(g):
            @pl.loop(1, devices)
            def _(i):
                spread(j, g, i).wait_recv()

            for k in range(batch):
                s = g * batch + k
                work_ref[s] = left_by(a_ref, got_ref[j, :, s].reshape(extent, columns))

        @pl.loop(0, extent // 8)
        def _(step):
            here = pl.ds(pl.multiple_of(step * 8, 8), 8)
            square = ka_ref[here, :] + kb_ref[...] + kz_ref[j * devices + me]
            weights = [jnp.exp(-width_ref[m] * square) for m in range(terms)]
            values = [work_ref[t, here, :] for t in range(sites)]
            for s in range(sites):
                total = values[s]
                for t in range(sites):
                    factor = amp_ref[s * sites + t] * weights[0]
                    for m in range(1, terms):
                        factor = factor + amp_ref[(m * sites + s) * sites + t] * weights[m]
                    total = total + factor * values[t]
                work_ref[s, here, :] = total

        @pl.loop(0, batches)
        def _(g):
            for k in range(batch):
                s = g * batch + k
                back_ref[j, :, s] = left_by(a_ref, work_ref[s]).reshape(devices, rows, columns)

            @pl.loop(1, devices)
            def _(i):
                restore(j, g, i).start()

        keep(j).start()

    @pl.loop(0, chunks)
    def _(j):
        keep(j).wait()

        @pl.loop(0, batches)
        def _(g):
            @pl.loop(1, devices)
            def _(i):
                spread(j, g, i).wait_send()
                restore(j, g, i).wait()


def tail_kernel(species_ref, charge_ref, *refs):
    parts_ref, x_ref, lj_ref, pot_ref, b_ref, z_ref, total_ref, next_ref, sum_ref = refs
    site = pl.program_id(0)
    rows, depth, columns = x_ref.shape[1:]
    chunks, devices = parts_ref.shape[:2]
    group = z_ref.shape[1] // depth

    @pl.when(site == 0)
    def _():
        sum_ref[...] = jnp.zeros_like(sum_ref)

    charge = charge_ref[site]
    for i in range(rows // group):
        here = slice(i * group, (i + 1) * group)
        joined = parts_ref[:, :, 0, here, :].reshape(chunks * devices * group, columns)
        total = right_by(left_by(z_ref, joined), b_ref).reshape(group, depth, columns)
        before = x_ref[0, here]
        indirect = total - before
        shifted = indirect - (lj_ref[0, here] + charge * pot_ref[here])
        after = jnp.where(shifted < 0, jnp.exp(jnp.minimum(shifted, 0.0)) - 1.0, shifted) - indirect
        change = after - before
        total_ref[0, here] = total
        next_ref[0, here] = after
        sum_ref[...] += jnp.sum((change * change).reshape(-1, 8, columns), axis=0)


def gather_kernel(sum_ref, out_ref, mine_ref, slots_ref, send_sem, recv_sem):
    devices = slots_ref.shape[0]
    me = lax.axis_index("slab")
    barrier = pltpu.get_barrier_semaphore()
    for i in range(1, devices):
        pl.semaphore_signal(barrier, inc=1, device_id={"slab": lax.rem(me + i, devices)})
    total = sum_ref[:, :128]
    for i in range(1, sum_ref.shape[1] // 128):
        total = total + sum_ref[:, i * 128:(i + 1) * 128]
    mine_ref[...] = total
    slots_ref[me] = total
    pl.semaphore_wait(barrier, devices - 1)
    copies = []
    for i in range(1, devices):
        copy = pltpu.make_async_remote_copy(
            src_ref=mine_ref,
            dst_ref=slots_ref.at[me],
            send_sem=send_sem.at[i],
            recv_sem=recv_sem.at[i],
            device_id={"slab": lax.rem(me + i, devices)},
        )
        copy.start()
        copies.append(copy)
    for copy in copies:
        copy.wait()
    out_ref[...] = jnp.sum(slots_ref[...], axis=0)


def plain_mix(values, square, chi_amp, chi_width):
    weight = jnp.exp(-chi_width.reshape((-1,) + (1,) * square.ndim) * square[None])
    scaled = weight[:, None] * values[None]
    return values + jnp.einsum("mab,mb...->a...", chi_amp, scaled, precision=precise)


def convolved_plain(x, chi_amp, chi_width, me, devices):
    sites, rows, depth, columns = x.shape
    extent = rows * devices
    b_table = jnp.asarray(hartley(columns), f32)
    z_table = jnp.asarray(hartley(depth), f32)
    a_table = jnp.asarray(hartley(extent), f32)
    y = jnp.einsum("sazb,bk->sazk", x, b_table, precision=precise)
    y = jnp.einsum("sazk,zl->salk", y, z_table, precision=precise)
    share = depth * columns // devices
    y = y.reshape(sites, rows, devices, share).transpose(2, 0, 1, 3)
    y = lax.all_to_all(y, "slab", split_axis=0, concat_axis=0)
    y = jnp.einsum("dsrc,drk->skc", y, a_table.reshape(devices, rows, extent), precision=precise)
    plane = (signed_square(depth)[:, None] + signed_square(columns)[None, :]).reshape(devices, share)
    mine = lax.dynamic_index_in_dim(jnp.asarray(plane), me, 0, keepdims=False)
    square = jnp.asarray(signed_square(extent))[:, None] + mine[None, :]
    y = plain_mix(y, square, chi_amp, chi_width)
    y = jnp.einsum("skc,drk->dsrc", y, a_table.reshape(devices, rows, extent), precision=precise)
    y = lax.all_to_all(y, "slab", split_axis=0, concat_axis=0)
    y = y.transpose(1, 2, 0, 3).reshape(sites, rows, depth, columns)
    y = jnp.einsum("salk,zl->sazk", y, z_table, precision=precise)
    return jnp.einsum("sazk,bk->sazb", y, b_table, precision=precise)


def closure_plain(total_corr, correlation, lj_field, potential, species, charges):
    indirect = total_corr - correlation
    energy = lj_field[species] + charges.astype(f32)[:, None, None, None] * potential[None]
    shifted = indirect - energy
    next_corr = jnp.where(shifted < 0, jnp.expm1(jnp.minimum(shifted, 0.0)), shifted) - indirect
    change = next_corr - correlation
    return next_corr, change * change


vmem = pl.BlockSpec(memory_space=pltpu.VMEM)
smem = pl.BlockSpec(memory_space=pltpu.SMEM)
limit = 56 * 1024 * 1024


def body(correlation, lj_field, potential, species, charges, chi_amp, chi_width):
    sites, rows, depth, columns = correlation.shape
    devices = lax.axis_size("slab")
    me = lax.axis_index("slab")
    extent = rows * devices
    cells = sites * extent * depth * columns

    if depth % devices or rows % 8 or columns % 128:
        total_corr = convolved_plain(correlation, chi_amp, chi_width, me, devices)
        next_corr, squares = closure_plain(
            total_corr, correlation, lj_field, potential, species, charges
        )
        summed = lax.psum(jnp.sum(squares), "slab")
        return (total_corr, next_corr, jnp.sqrt(summed / cells + 1e-06).reshape(1))

    group = 8
    chunks = depth // devices
    z_basis = hartley(depth)
    forward = np.einsum("kz,ab->kabz", z_basis, np.eye(group)).reshape(group * depth, group * depth)
    b_table = halves(hartley(columns))
    a_table = halves(hartley(extent))
    z_table = halves(forward)
    z_back = halves(forward.T)
    b_spec = pl.BlockSpec((2, columns, columns), lambda s, *_: (0, 0, 0))
    z_spec = pl.BlockSpec((2, group * depth, group * depth), lambda s, *_: (0, 0, 0))
    row_spec = pl.BlockSpec((1, rows, depth, columns), lambda s, *_: (s, 0, 0, 0))
    part_spec = pl.BlockSpec(
        (chunks, devices, 1, rows, columns), lambda s, *_: (0, 0, s, 0, 0)
    )
    whole = (chunks, devices, sites, rows, columns)
    size = correlation.size
    batches = 4 if sites % 4 == 0 else 1
    pairs = pltpu.SemaphoreType.DMA((chunks, batches, devices))

    kz = jnp.asarray(signed_square(depth))
    ka = jnp.asarray(np.repeat(signed_square(extent)[:, None], columns, axis=1))
    kb = jnp.asarray(np.repeat(signed_square(columns)[None, :], 8, axis=0))
    arrived = pl.pallas_call(
        core_kernel,
        in_specs=[smem, smem, smem] + [vmem] * 6,
        out_specs=pl.BlockSpec(memory_space=pl.ANY),
        out_shape=jax.ShapeDtypeStruct(whole, f32),
        scratch_shapes=[
            pltpu.VMEM(whole, f32),
            pltpu.VMEM(whole, f32),
            pltpu.VMEM((sites, extent, columns), f32),
            pltpu.VMEM(whole, f32),
            pairs,
            pairs,
            pairs,
            pairs,
            pltpu.SemaphoreType.DMA((chunks,)),
        ],
        compiler_params=pltpu.CompilerParams(
            collective_id=1, has_side_effects=True, vmem_limit_bytes=limit
        ),
        name="core",
    )(chi_amp.reshape(-1), chi_width, kz, correlation, b_table, z_table, a_table, ka, kb)

    total_corr, next_corr, sums = pl.pallas_call(
        tail_kernel,
        grid_spec=pltpu.PrefetchScalarGridSpec(
            num_scalar_prefetch=2,
            grid=(sites,),
            in_specs=[
                part_spec,
                row_spec,
                pl.BlockSpec((1, rows, depth, columns), lambda s, kind, _: (kind[s], 0, 0, 0)),
                pl.BlockSpec((rows, depth, columns), lambda s, *_: (0, 0, 0)),
                b_spec,
                z_spec,
            ],
            out_specs=[row_spec, row_spec, pl.BlockSpec((8, columns), lambda s, *_: (0, 0))],
        ),
        out_shape=[
            jax.ShapeDtypeStruct(correlation.shape, f32),
            jax.ShapeDtypeStruct(correlation.shape, f32),
            jax.ShapeDtypeStruct((8, columns), f32),
        ],
        compiler_params=pltpu.CompilerParams(vmem_limit_bytes=limit),
        cost_estimate=pl.CostEstimate(
            flops=12 * size * columns, bytes_accessed=20 * size, transcendentals=size
        ),
        name="tail",
    )(species, charges.astype(f32), arrived, correlation, lj_field, potential, b_table, z_back)
    gathered = pl.pallas_call(
        gather_kernel,
        in_specs=[vmem],
        out_specs=vmem,
        out_shape=jax.ShapeDtypeStruct((8, 128), f32),
        scratch_shapes=[
            pltpu.VMEM((8, 128), f32),
            pltpu.VMEM((devices, 8, 128), f32),
            pltpu.SemaphoreType.DMA((devices,)),
            pltpu.SemaphoreType.DMA((devices,)),
        ],
        compiler_params=pltpu.CompilerParams(collective_id=0, has_side_effects=True),
        name="gather",
    )(sums)
    summed = jnp.sum(gathered)
    return (total_corr, next_corr, jnp.sqrt(summed / cells + 1e-06).reshape(1))


def solution(mesh):
    placed = (
        P("sys", "slab", None, None),
        P("sys", "slab", None, None),
        P(("sys", "slab"), None, None),
        P(),
        P(),
        P(),
        P(),
    )
    return jax.shard_map(
        body,
        mesh=mesh,
        in_specs=placed,
        out_specs=(P("sys", "slab", None, None), P("sys", "slab", None, None), P("sys")),
        check_vma=False,
    )
```
